32 devices in a mesh: dp: 8 (over y, x, core), mp: 4 (over z).
Axes of the slice: x: 2, y: 2, z: 4, core: 2. Of those that a mesh axis runs over, the one named last changes fastest.
Arguments:
- layer_inputs: bfloat16 [2, 3072, 1024], P(None, 'dp'), may hold values from -11 to 11, as said below
- out_grads: bfloat16 [2, 3072, 1024], P(None, 'dp'), may hold values from -11 to 11, as said below
- damping: float32 [4], replicated, may hold values from 0.1 to 0.5
- owners: int32 [4], replicated, may hold values from 0 to 8, as said below
- old_inverse: bfloat16 [4, 1024, 1024], P('mp'), may hold values from -1.5 to 1.5, as said below
- step_size: float32 [2], replicated, may hold values from 100 to 400
Outputs:
- updates: bfloat16 [2, 1024, 1024], P(None, 'dp')
The draws below stay inside these ranges and needn't reach their ends.
Inputs may be any that keep to these rules, and one draw needn't show every extreme that they name: `layer_inputs`: layer inputs: rows of mixed scale. `out_grads`: output gradients: rows of mixed scale. `old_inverse`: each kept inverse is symmetric. `owners`: exactly one factor has the value 8.
All inputs are finite; a program needn't handle non-finite values.
Results may differ from the reference program's by a relative error of at most 0.012.
Values may be sent and summed in bfloat16 or wider, within the bound.
A program may use at most 128 MiB of HBM per device.

```python
import math
import jax
import jax.numpy as jnp
from jax import lax

D = 1024
LAYERS = 2
FACTORS = 4
TOKENS = 3072
N_DP = 8


def rough_rows(key):
    first, second = jax.random.split(key, 2)
    base = jnp.clip(jax.random.normal(first, (LAYERS, TOKENS, D), jnp.float32), -5.0, 5.0)
    ramp = 0.5 + jnp.arange(TOKENS, dtype=jnp.float32) / TOKENS
    rough = jax.random.uniform(second, (LAYERS, TOKENS, 1), jnp.float32, 0.7, 1.4)
    return jnp.clip(base * ramp[None, :, None] * rough, -10.5, 10.5)


def draw_layer_inputs(key, part):
    return rough_rows(jax.random.fold_in(key, 11)).astype(jnp.bfloat16)


def draw_out_grads(key, part):
    return rough_rows(jax.random.fold_in(key, 23)).astype(jnp.bfloat16)


def draw_owners(key, part):
    first, second = jax.random.split(jax.random.fold_in(key, 51), 2)
    chosen = jax.random.randint(first, (FACTORS,), 0, N_DP)
    kept_slot = jax.random.randint(second, (), 0, FACTORS)
    zero_slot = (kept_slot + 1) % FACTORS
    slots = jnp.arange(FACTORS, dtype=jnp.int32)
    chosen = jnp.where(slots == zero_slot, 0, chosen)
    return jnp.where(slots == kept_slot, N_DP, chosen).astype(jnp.int32)


def draw_old_inverse(key, part):
    first, second = jax.random.split(jax.random.fold_in(key, 37))
    noise = jax.random.normal(first, (FACTORS, D, D), jnp.float32) * (0.4 / D ** 0.5)
    noise = jnp.clip(noise, -0.5, 0.5)
    symmetric = 0.5 * (noise + jnp.swapaxes(noise, 1, 2))
    diagonal = jnp.exp(jax.random.uniform(second, (FACTORS, D), jnp.float32, jnp.log(0.5), jnp.log(1.0)))
    identity = jnp.eye(D, dtype=jnp.float32)
    return (symmetric + diagonal[:, :, None] * identity[None]).astype(jnp.bfloat16)


def setup_inputs(seed: int = 0) -> dict:
    seeds = jax.random.split(jax.random.key(seed), 7)
    layer_inputs = draw_layer_inputs(jax.random.fold_in(seeds[6], 71), 0)
    out_grads = draw_out_grads(jax.random.fold_in(seeds[6], 71), 0)
    damping = jnp.clip(jnp.exp(jax.random.uniform(seeds[2], (FACTORS,), jnp.float32, math.log(0.1), math.log(0.5))), 0.1, 0.5)
    owners = draw_owners(jax.random.fold_in(seeds[6], 71), 0)
    old_inverse = draw_old_inverse(jax.random.fold_in(seeds[6], 71), 0)
    step_size = jnp.clip(jnp.exp(jax.random.uniform(seeds[5], (LAYERS,), jnp.float32, math.log(100.0), math.log(400.0))), 100.0, 400.0)
    return dict(layer_inputs=layer_inputs, out_grads=out_grads, damping=damping, owners=owners, old_inverse=old_inverse, step_size=step_size)


def invert_damped(factor, shift):
    identity = jnp.eye(factor.shape[0], dtype=factor.dtype)
    lower = jnp.linalg.cholesky(factor + shift * identity)
    return jax.scipy.linalg.cho_solve((lower, True), identity).astype(jnp.bfloat16)

def reference(layer_inputs, out_grads, damping, owners, old_inverse, step_size):
    count_all = layer_inputs.shape[1]
    highest = lax.Precision.HIGHEST
    inverses = []
    for layer in range(LAYERS):
        inputs_wide = layer_inputs[layer].astype(jnp.float32)
        grads_wide = out_grads[layer].astype(jnp.float32)
        for which, source_rows in ((0, inputs_wide), (1, grads_wide)):
            factor_id = 2 * layer + which
            factor = jnp.dot(source_rows.T, source_rows, precision=highest) / count_all
            computed = invert_damped(factor, damping[factor_id])
            inverses.append(jnp.where(owners[factor_id] < N_DP, computed, old_inverse[factor_id]))
    results = []
    for layer in range(LAYERS):
        inputs_wide = layer_inputs[layer].astype(jnp.float32)
        grads_wide = out_grads[layer].astype(jnp.float32)
        gradient = jnp.dot(grads_wide.T, inputs_wide, precision=highest) / count_all
        gradient_low = gradient.astype(jnp.bfloat16)
        half = jnp.dot(gradient_low.astype(jnp.float32), inverses[2 * layer].astype(jnp.float32), precision=highest).astype(jnp.bfloat16)
        product = jnp.dot(inverses[2 * layer + 1].astype(jnp.float32), half.astype(jnp.float32), precision=highest)
        results.append((step_size[layer] * product).astype(jnp.bfloat16))
    return jnp.stack(results)
```

```python
import functools
import jax
import jax.numpy as jnp
from jax import lax
from jax.experimental import pallas as pl
from jax.experimental.pallas import tpu as pltpu
from jax.sharding import PartitionSpec as P

F32 = jnp.float32
BF16 = jnp.bfloat16
MESH = pl.DeviceIdType.MESH
HI = lax.Precision.HIGHEST
BLOCK = 128
TILE = 8


def remote(src, dst, send, recv, where):
    return pltpu.make_async_remote_copy(
        src_ref=src, dst_ref=dst, send_sem=send, recv_sem=recv,
        device_id=where, device_id_type=MESH,
    )


def gather_kernel(n, x, y, gx, gy, loc, s1, r1, s2, r2, s3, r3):
    me = lax.axis_index("dp")
    m = lax.axis_index("mp")
    half = n // 2
    pair, side = me // 2, me % 2
    sibling = pair * 2 + 1 - side
    barrier = pltpu.get_barrier_semaphore()
    for s in range(1, n):
        pl.semaphore_signal(barrier, inc=1, device_id=((me + s) % n, m), device_id_type=MESH)
    pl.semaphore_wait(barrier, n - 1)

    sent = []
    for s in range(1, half):
        peer = ((pair + s) % half) * 2 + side
        c = remote(x, gx.at[me], s1.at[s], r1.at[s], (peer, m))
        c.start()
        sent.append(c)
    own = remote(x, gx.at[me], s1.at[0], r1.at[0], (sibling, m))
    own.start()
    sent.append(own)
    blocks = []
    for s in range(1, n):
        peer = (me + s) % n
        c = remote(y.at[peer], gy.at[me], s3.at[s], r3.at[s], (peer, m))
        c.start()
        sent.append(c)
        blocks.append((s, (me - s + n) % n))
    here = pltpu.make_async_copy(x, gx.at[me], loc.at[0])
    here.start()
    here_y = pltpu.make_async_copy(y.at[me], gy.at[me], loc.at[1])
    here_y.start()
    for s in range(1, half):
        origin = ((pair - s + half) % half) * 2 + side
        remote(x, gx.at[origin], s1.at[s], r1.at[s], (sibling, m)).wait_recv()
        c = remote(gx.at[origin], gx.at[origin], s2.at[s], r2.at[s], (sibling, m))
        c.start()
        sent.append(c)
    remote(x, gx.at[sibling], s1.at[0], r1.at[0], (sibling, m)).wait_recv()
    for s in range(1, half):
        origin = ((pair - s + half) % half) * 2 + 1 - side
        remote(x, gx.at[origin], s2.at[s], r2.at[s], (sibling, m)).wait_recv()
    for s, origin in blocks:
        remote(y.at[origin], gy.at[origin], s3.at[s], r3.at[s], (origin, m)).wait_recv()
    for c in sent:
        c.wait_send()
    here.wait()
    here_y.wait()


def gather(n, x, y):
    any_space = pl.BlockSpec(memory_space=pl.ANY)
    dma = pltpu.SemaphoreType.DMA
    return pl.pallas_call(
        functools.partial(gather_kernel, n),
        out_shape=[
            jax.ShapeDtypeStruct((n,) + x.shape, x.dtype),
            jax.ShapeDtypeStruct(y.shape, y.dtype),
        ],
        in_specs=[any_space] * 2,
        out_specs=[any_space] * 2,
        scratch_shapes=[dma((2,)), dma((n,)), dma((n,)), dma((n,)), dma((n,)), dma((n,)), dma((n,))],
        compiler_params=pltpu.CompilerParams(collective_id=0, has_side_effects=True),
        name="gather_sources",
    )(x, y)


def sweep_block(tiles):
    width = tiles[0].shape[1]
    lane = lax.broadcasted_iota(jnp.int32, (TILE, width), 1)
    sub = lax.broadcasted_iota(jnp.int32, (TILE, width), 0)
    for k in range(width):
        kt, ks = divmod(k, TILE)
        row = jnp.broadcast_to(tiles[kt][ks : ks + 1, :], (TILE, width))
        pivot = jnp.broadcast_to(row[:, k : k + 1], (TILE, width))
        inv = 1.0 / pivot
        at = lane == k
        scaled = jnp.where(at, -inv, row * inv)
        out = []
        for t, tile in enumerate(tiles):
            col = jnp.broadcast_to(tile[:, k : k + 1], (TILE, width))
            new = jnp.where(at, 0.0, tile) - col * scaled
            if t == kt:
                new = jnp.where(sub == ks, scaled, new)
            out.append(new)
        tiles = out
    return tiles


def invert_kernel(refreshed, shift, factor, kept, out, a, r, p):
    width = factor.shape[0]
    steps = width // BLOCK
    row_id = lax.broadcasted_iota(jnp.int32, (BLOCK, width), 0)
    col_id = lax.broadcasted_iota(jnp.int32, (BLOCK, width), 1)

    @pl.loop(0, steps)
    def _(i):
        rows = pl.ds(pl.multiple_of(i * BLOCK, BLOCK), BLOCK)
        a[rows, :] = factor[rows, :] + jnp.where(row_id + i * BLOCK == col_id, shift[0], 0.0)

    @pl.loop(0, steps)
    def _(k):
        ks = pl.ds(pl.multiple_of(k * BLOCK, BLOCK), BLOCK)
        block = a[ks, ks]
        tiles = [block[t * TILE : (t + 1) * TILE, :] for t in range(BLOCK // TILE)]
        tiles = sweep_block(tiles)
        for t, tile in enumerate(tiles):
            p[t * TILE : (t + 1) * TILE, :] = tile
        r[...] = -jnp.dot(p[...], a[ks, :], precision=HI, preferred_element_type=F32)

        @pl.loop(0, steps)
        def _(i):
            rows = pl.ds(pl.multiple_of(i * BLOCK, BLOCK), BLOCK)
            c = a[rows, ks]
            a[rows, :] = a[rows, :] - jnp.dot(c, r[...], precision=HI, preferred_element_type=F32)
            a[rows, ks] = -jnp.dot(c, p[...], precision=HI, preferred_element_type=F32)

        a[ks, :] = r[...]
        a[ks, ks] = p[...]

    fresh = refreshed[0] > 0

    @pl.loop(0, steps)
    def _(i):
        rows = pl.ds(pl.multiple_of(i * BLOCK, BLOCK), BLOCK)
        out[rows, :] = jnp.where(fresh, -a[rows, :], kept[rows, :].astype(F32)).astype(BF16)


def invert(refreshed, shift, factor, kept):
    width = factor.shape[0]
    smem = pl.BlockSpec(memory_space=pltpu.SMEM)
    vmem = pl.BlockSpec(memory_space=pltpu.VMEM)
    return pl.pallas_call(
        invert_kernel,
        out_shape=jax.ShapeDtypeStruct((width, width), BF16),
        in_specs=[smem, smem, vmem, vmem],
        out_specs=vmem,
        scratch_shapes=[
            pltpu.VMEM((width, width), F32),
            pltpu.VMEM((BLOCK, width), F32),
            pltpu.VMEM((BLOCK, BLOCK), F32),
        ],
        compiler_params=pltpu.CompilerParams(vmem_limit_bytes=40 * 1024 * 1024),
        name="invert_damped",
    )(refreshed, shift, factor, kept)


def apply_kernel(n, parts, inv, grad, step, out, b, got, done, s1, r1, s2, r2):
    me = lax.axis_index("dp")
    m = lax.axis_index("mp")
    other = m + 1 - 2 * (m % 2)
    width = inv.shape[0]
    rw = width // n
    is_out = m % 2
    barrier = pltpu.get_barrier_semaphore()
    for j in range(n):
        pl.semaphore_signal(barrier, inc=1, device_id=(j, other), device_id_type=MESH)
    for q in range(1, parts):
        pl.semaphore_signal(barrier, inc=1, device_id=(me, (m + q) % parts), device_id_type=MESH)
    pl.semaphore_wait(barrier, n + parts - 1)

    b[...] = jnp.dot(inv[...], grad[...], preferred_element_type=F32).astype(BF16).reshape(n, rw, rw)
    for s in range(n):
        j = (me + s) % n

        @pl.when(is_out == 1)
        def _():
            remote(b.at[j], got.at[me], s1.at[s], r1.at[s], (j, other)).start()

    @pl.when(is_out == 0)
    def _():
        for s in range(n):
            origin = (me - s + n) % n
            remote(b.at[origin], got.at[origin], s1.at[s], r1.at[s], (origin, other)).wait_recv()
        total = jnp.zeros((rw, width), F32)
        for j in range(n):
            total = total + jnp.dot(got[j], inv[j * rw : (j + 1) * rw, :], preferred_element_type=F32)
        done[m // 2] = (total * step[m // 2]).astype(BF16)
        for q in range(1, parts):
            remote(
                done.at[m // 2], done.at[m // 2], s2.at[q], r2.at[q], (me, (m + q) % parts)
            ).start()
        for q in range(1, parts):
            remote(
                done.at[m // 2], done.at[m // 2], s2.at[q], r2.at[q], (me, (m + q) % parts)
            ).wait_send()

    @pl.when(is_out == 1)
    def _():
        for s in range(n):
            j = (me + s) % n
            remote(b.at[j], got.at[me], s1.at[s], r1.at[s], (j, other)).wait_send()

    for q in range(1, parts):
        origin = (m - q + parts) % parts

        @pl.when(origin % 2 == 0)
        def _():
            slot = origin // 2
            remote(done.at[slot], done.at[slot], s2.at[q], r2.at[q], (me, origin)).wait_recv()

    out[...] = done[...]


def apply(n, parts, inv, grad, step):
    width = inv.shape[0]
    rw = width // n
    layers = step.shape[0]
    vmem = pl.BlockSpec(memory_space=pltpu.VMEM)
    dma = pltpu.SemaphoreType.DMA
    return pl.pallas_call(
        functools.partial(apply_kernel, n, parts),
        out_shape=jax.ShapeDtypeStruct((layers, rw, width), BF16),
        in_specs=[vmem, vmem, pl.BlockSpec(memory_space=pltpu.SMEM)],
        out_specs=vmem,
        scratch_shapes=[
            pltpu.VMEM((n, rw, rw), BF16),
            pltpu.VMEM((n, rw, rw), BF16),
            pltpu.VMEM((layers, rw, width), BF16),
            dma((n,)), dma((n,)), dma((parts,)), dma((parts,)),
        ],
        compiler_params=pltpu.CompilerParams(
            collective_id=1, has_side_effects=True, vmem_limit_bytes=32 * 1024 * 1024
        ),
        name="apply_inverses",
    )(inv, grad, step)


def body(layer_inputs, out_grads, damping, owners, old_inverse, step_size):
    parts = lax.axis_size("mp")
    n = lax.axis_size("dp")
    m = lax.axis_index("mp")
    tokens = layer_inputs.shape[1]
    width = layer_inputs.shape[2]
    count_all = tokens * n
    rw = width // n
    xs = lax.dynamic_index_in_dim(layer_inputs, m // 2, 0, keepdims=False)
    gs = lax.dynamic_index_in_dim(out_grads, m // 2, 0, keepdims=False)
    even = m % 2 == 0
    mine = jnp.where(even, xs, gs)
    other = jnp.where(even, gs, xs).reshape(tokens, n, rw).transpose(1, 0, 2)
    source, columns = gather(n, mine, other)
    source = source.reshape(count_all, width)
    columns = columns.reshape(count_all, rw)
    dims = (((0,), (0,)), ((), ()))
    factor = lax.dot_general(source, source, dims, preferred_element_type=F32) / count_all
    grad = (lax.dot_general(source, columns, dims, preferred_element_type=F32) / count_all).astype(BF16)
    refreshed = (owners[m] < n).astype(jnp.int32).reshape(1)
    shift = damping[m].reshape(1)
    inverse = invert(refreshed, shift, factor, old_inverse[0])
    return apply(n, parts, inverse, grad, step_size)


def solution(mesh):
    placed = (P(None, "dp", None), P(None, "dp", None), P(), P(), P("mp", None, None), P())
    return jax.shard_map(
        body, mesh=mesh, in_specs=placed, out_specs=P(None, "dp", None), check_vma=False
    )
```

```python
import functools
import jax
import jax.numpy as jnp
from jax import lax
from jax.experimental import pallas as pl
from jax.experimental.pallas import tpu as pltpu
from jax.sharding import PartitionSpec as P

F32 = jnp.float32
BF16 = jnp.bfloat16
MESH = pl.DeviceIdType.MESH
HI = lax.Precision.HIGHEST
BLOCK = 128
TILE = 8


def remote(src, dst, send, recv, where):
    return pltpu.make_async_remote_copy(
        src_ref=src, dst_ref=dst, send_sem=send, recv_sem=recv,
        device_id=where, device_id_type=MESH,
    )


def gather_kernel(n, direct, a_ref, b_ref, gx, gy, loc, s1, r1, s2, r2, s3, r3):
    me = lax.axis_index("dp")
    m = lax.axis_index("mp")
    half = n // 2
    pair, side = me // 2, me % 2
    sibling = pair * 2 + 1 - side
    barrier = pltpu.get_barrier_semaphore()
    for s in range(1, n):
        pl.semaphore_signal(barrier, inc=1, device_id=((me + s) % n, m), device_id_type=MESH)
    pl.semaphore_wait(barrier, n - 1)

    def begin(x, part):
        for s in range(1, half):
            peer = ((pair + s) % half) * 2 + side
            remote(x, gx.at[me], s1.at[s], r1.at[s], (peer, m)).start()
        remote(x, gx.at[me], s1.at[0], r1.at[0], (sibling, m)).start()
        for s in range(1, n):
            peer = (me + s) % n
            remote(part(peer), gy.at[me], s3.at[s], r3.at[s], (peer, m)).start()
        pltpu.make_async_copy(x, gx.at[me], loc.at[0]).start()
        pltpu.make_async_copy(part(me), gy.at[me], loc.at[1]).start()

    if direct:
        layer = m // 2
        rw = gy.shape[2]

        def columns(ref):
            return lambda j: ref.at[layer, :, pl.ds(pl.multiple_of(j * rw, rw), rw)]

        @pl.when(m % 2 == 0)
        def _():
            begin(a_ref.at[layer], columns(b_ref))

        @pl.when(m % 2 == 1)
        def _():
            begin(b_ref.at[layer], columns(a_ref))
    else:
        begin(a_ref, lambda j: b_ref.at[j])

    x = gx.at[me]
    for s in range(1, half):
        origin = ((pair - s + half) % half) * 2 + side
        remote(x, gx.at[origin], s1.at[s], r1.at[s], (sibling, m)).wait_recv()
        remote(gx.at[origin], gx.at[origin], s2.at[s], r2.at[s], (sibling, m)).start()
    remote(x, gx.at[sibling], s1.at[0], r1.at[0], (sibling, m)).wait_recv()
    for s in range(1, half):
        origin = ((pair - s + half) % half) * 2 + 1 - side
        remote(x, gx.at[origin], s2.at[s], r2.at[s], (sibling, m)).wait_recv()
    for s in range(1, n):
        origin = (me - s + n) % n
        remote(gy.at[me], gy.at[origin], s3.at[s], r3.at[s], (origin, m)).wait_recv()
    for s in range(half):
        remote(x, x, s1.at[s], r1.at[s], (sibling, m)).wait_send()
    for s in range(1, half):
        remote(x, x, s2.at[s], r2.at[s], (sibling, m)).wait_send()
    for s in range(1, n):
        remote(gy.at[me], gy.at[me], s3.at[s], r3.at[s], (sibling, m)).wait_send()
    pltpu.make_async_copy(x, x, loc.at[0]).wait()
    pltpu.make_async_copy(gy.at[me], gy.at[me], loc.at[1]).wait()


def gather(n, direct, x, y):
    any_space = pl.BlockSpec(memory_space=pl.ANY)
    dma = pltpu.SemaphoreType.DMA
    return pl.pallas_call(
        functools.partial(gather_kernel, n, direct),
        out_shape=[
            jax.ShapeDtypeStruct((n,) + x.shape[-2:], x.dtype),
            jax.ShapeDtypeStruct((n, x.shape[-2], x.shape[-1] // n), y.dtype),
        ],
        in_specs=[any_space] * 2,
        out_specs=[any_space] * 2,
        scratch_shapes=[dma((2,)), dma((n,)), dma((n,)), dma((n,)), dma((n,)), dma((n,)), dma((n,))],
        compiler_params=pltpu.CompilerParams(collective_id=0, has_side_effects=True),
        name="gather_sources",
    )(x, y)


def sweep_block(tiles):
    width = tiles[0].shape[1]
    shape = (TILE, width)
    lane = lax.broadcasted_iota(jnp.int32, shape, 1)
    sub = lax.broadcasted_iota(jnp.int32, shape, 0)
    idx = range(TILE)
    for g in range(width // TILE):
        first = g * TILE
        inside = (lane >= first) & (lane < first + TILE)
        rows = [jnp.broadcast_to(tiles[g][i : i + 1, :], shape) for i in idx]
        s = {
            (i, j): jnp.broadcast_to(rows[i][:, first + j : first + j + 1], shape)
            for i in idx for j in idx if i <= j
        }

        def at(i, j):
            return (i, j) if i <= j else (j, i)

        for k in idx[::2]:
            h = k + 1
            inv = 1.0 / (s[k, k] * s[h, h] - s[k, h] * s[k, h])
            p00, p01, p11 = s[h, h] * inv, -s[k, h] * inv, s[k, k] * inv
            rest = [i for i in idx if i not in (k, h)]
            u = {i: s[at(i, k)] * p00 + s[at(i, h)] * p01 for i in rest}
            v = {i: s[at(i, k)] * p01 + s[at(i, h)] * p11 for i in rest}
            for i in rest:
                for j in rest:
                    if i <= j:
                        s[i, j] = s[i, j] - (s[at(i, k)] * u[j] + s[at(i, h)] * v[j])
            for i in rest:
                s[at(i, k)] = u[i]
                s[at(i, h)] = v[i]
            s[k, k], s[k, h], s[h, h] = -p00, -p01, -p11
        rows = [
            jnp.where(inside, jnp.where(lane == first + i, -1.0, 0.0), rows[i]) for i in idx
        ]
        scaled = []
        for i in idx:
            terms = [s[at(i, j)] * rows[j] for j in idx]
            while len(terms) > 1:
                terms = [x + y for x, y in zip(terms[0::2], terms[1::2])]
            scaled.append(-terms[0])
        out = []
        for t, tile in enumerate(tiles):
            if t == g:
                fresh = scaled[0]
                for i in idx[1:]:
                    fresh = jnp.where(sub == i, scaled[i], fresh)
                out.append(fresh)
                continue
            terms = [
                jnp.broadcast_to(tile[:, first + i : first + i + 1], shape) * scaled[i] for i in idx
            ]
            while len(terms) > 1:
                terms = [x + y for x, y in zip(terms[0::2], terms[1::2])]
            out.append(jnp.where(inside, 0.0, tile) - terms[0])
        tiles = out
    return tiles


def invert_kernel(refreshed, shift, factor, kept, out, a, r, p):
    width = factor.shape[0]
    steps = width // BLOCK
    row_id = lax.broadcasted_iota(jnp.int32, (BLOCK, width), 0)
    col_id = lax.broadcasted_iota(jnp.int32, (BLOCK, width), 1)

    @pl.loop(0, steps)
    def _(i):
        rows = pl.ds(pl.multiple_of(i * BLOCK, BLOCK), BLOCK)
        a[rows, :] = factor[rows, :] + jnp.where(row_id + i * BLOCK == col_id, shift[0], 0.0)

    @pl.loop(0, steps)
    def _(k):
        ks = pl.ds(pl.multiple_of(k * BLOCK, BLOCK), BLOCK)
        block = a[ks, ks]
        tiles = [block[t * TILE : (t + 1) * TILE, :] for t in range(BLOCK // TILE)]
        tiles = sweep_block(tiles)
        for t, tile in enumerate(tiles):
            p[t * TILE : (t + 1) * TILE, :] = tile
        r[...] = -jnp.dot(p[...], a[ks, :], precision=HI, preferred_element_type=F32)
        r[:, ks] = p[...]

        @pl.loop(0, steps)
        def _(i):
            rows = pl.ds(pl.multiple_of(i * BLOCK, BLOCK), BLOCK)
            c = a[rows, ks]
            a[rows, ks] = jnp.zeros((BLOCK, BLOCK), F32)
            a[rows, :] = a[rows, :] - jnp.dot(c, r[...], precision=HI, preferred_element_type=F32)

        a[ks, :] = r[...]

    fresh = refreshed[0] > 0

    @pl.loop(0, steps)
    def _(i):
        rows = pl.ds(pl.multiple_of(i * BLOCK, BLOCK), BLOCK)
        out[rows, :] = jnp.where(fresh, -a[rows, :], kept[rows, :].astype(F32)).astype(BF16)


def invert(refreshed, shift, factor, kept):
    width = factor.shape[0]
    smem = pl.BlockSpec(memory_space=pltpu.SMEM)
    vmem = pl.BlockSpec(memory_space=pltpu.VMEM)
    return pl.pallas_call(
        invert_kernel,
        out_shape=jax.ShapeDtypeStruct((width, width), BF16),
        in_specs=[smem, smem, vmem, vmem],
        out_specs=vmem,
        scratch_shapes=[
            pltpu.VMEM((width, width), F32),
            pltpu.VMEM((BLOCK, width), F32),
            pltpu.VMEM((BLOCK, BLOCK), F32),
        ],
        compiler_params=pltpu.CompilerParams(vmem_limit_bytes=40 * 1024 * 1024),
        name="invert_damped",
    )(refreshed, shift, factor, kept)


def apply_kernel(n, parts, inv, grad, step, out, b, got, done, s1, r1, s2, r2):
    me = lax.axis_index("dp")
    m = lax.axis_index("mp")
    other = m + 1 - 2 * (m % 2)
    width = inv.shape[0]
    rw = width // n
    is_out = m % 2
    barrier = pltpu.get_barrier_semaphore()
    for j in range(n):
        pl.semaphore_signal(barrier, inc=1, device_id=(j, other), device_id_type=MESH)
    for q in range(1, parts):
        pl.semaphore_signal(barrier, inc=1, device_id=(me, (m + q) % parts), device_id_type=MESH)
    pl.semaphore_wait(barrier, n + parts - 1)

    b[...] = jnp.dot(inv[...], grad[...], preferred_element_type=F32).astype(BF16).reshape(n, rw, rw)
    for s in range(n):
        j = (me + s) % n

        @pl.when(is_out == 1)
        def _():
            remote(b.at[j], got.at[me], s1.at[s], r1.at[s], (j, other)).start()

    @pl.when(is_out == 0)
    def _():
        for s in range(n):
            origin = (me - s + n) % n
            remote(b.at[origin], got.at[origin], s1.at[s], r1.at[s], (origin, other)).wait_recv()
        total = jnp.zeros((rw, width), F32)
        for j in range(n):
            total = total + jnp.dot(got[j], inv[j * rw : (j + 1) * rw, :], preferred_element_type=F32)
        done[m // 2] = (total * step[m // 2]).astype(BF16)

    chunks = max(1, min(4, rw // 16))
    size = rw // chunks

    def hop(layer, c, way, where):
        part = done.at[layer, pl.ds(c * size, size)]
        return remote(part, part, s2.at[layer, way, c], r2.at[layer, c], (me, where))

    up, down = m + 1, m - 1
    for c in range(chunks):
        for s in range(0, parts, 2):
            layer = s // 2

            @pl.when((m == s) & (up < parts))
            def _():
                hop(layer, c, 0, up).start()

            @pl.when((m == s) & (down >= 0))
            def _():
                hop(layer, c, 1, down).start()

    for c in range(chunks):
        for s in range(0, parts, 2):
            layer = s // 2

            @pl.when(m != s)
            def _():
                hop(layer, c, 0, other).wait_recv()

            @pl.when((m > s) & (up < parts))
            def _():
                hop(layer, c, 0, up).start()

            @pl.when((m < s) & (down >= 0))
            def _():
                hop(layer, c, 1, down).start()

    for c in range(chunks):
        for s in range(0, parts, 2):
            layer = s // 2

            @pl.when((m >= s) & (up < parts))
            def _():
                hop(layer, c, 0, other).wait_send()

            @pl.when((m <= s) & (down >= 0))
            def _():
                hop(layer, c, 1, other).wait_send()

    @pl.when(is_out == 1)
    def _():
        for s in range(n):
            j = (me + s) % n
            remote(b.at[j], got.at[me], s1.at[s], r1.at[s], (j, other)).wait_send()

    out[...] = done[...]


def apply(n, parts, inv, grad, step):
    width = inv.shape[0]
    rw = width // n
    layers = step.shape[0]
    vmem = pl.BlockSpec(memory_space=pltpu.VMEM)
    dma = pltpu.SemaphoreType.DMA
    return pl.pallas_call(
        functools.partial(apply_kernel, n, parts),
        out_shape=jax.ShapeDtypeStruct((layers, rw, width), BF16),
        in_specs=[vmem, vmem, pl.BlockSpec(memory_space=pltpu.SMEM)],
        out_specs=vmem,
        scratch_shapes=[
            pltpu.VMEM((n, rw, rw), BF16),
            pltpu.VMEM((n, rw, rw), BF16),
            pltpu.VMEM((layers, rw, width), BF16),
            dma((n,)), dma((n,)), dma((layers, 2, 4)), dma((layers, 4)),
        ],
        compiler_params=pltpu.CompilerParams(
            collective_id=1, has_side_effects=True, vmem_limit_bytes=32 * 1024 * 1024
        ),
        name="apply_inverses",
    )(inv, grad, step)


def body(layer_inputs, out_grads, damping, owners, old_inverse, step_size):
    parts = lax.axis_size("mp")
    n = lax.axis_size("dp")
    m = lax.axis_index("mp")
    tokens = layer_inputs.shape[1]
    width = layer_inputs.shape[2]
    count_all = tokens * n
    rw = width // n
    direct = rw % 128 == 0
    if direct:
        mine, other = layer_inputs, out_grads
    else:
        xs = lax.dynamic_index_in_dim(layer_inputs, m // 2, 0, keepdims=False)
        gs = lax.dynamic_index_in_dim(out_grads, m // 2, 0, keepdims=False)
        even = m % 2 == 0
        mine = jnp.where(even, xs, gs)
        other = jnp.where(even, gs, xs).reshape(tokens, n, rw).transpose(1, 0, 2)
    source, columns = gather(n, direct, mine, other)
    source = source.reshape(count_all, width)
    columns = columns.reshape(count_all, rw)
    dims = (((0,), (0,)), ((), ()))
    factor = lax.dot_general(source, source, dims, preferred_element_type=F32) / count_all
    grad = (lax.dot_general(source, columns, dims, preferred_element_type=F32) / count_all).astype(BF16)
    refreshed = (owners[m] < n).astype(jnp.int32).reshape(1)
    shift = damping[m].reshape(1)
    inverse = invert(refreshed, shift, factor, old_inverse[0])
    return apply(n, parts, inverse, grad, step_size)


def solution(mesh):
    placed = (P(None, "dp", None), P(None, "dp", None), P(), P(), P("mp", None, None), P())
    return jax.shard_map(
        body, mesh=mesh, in_specs=placed, out_specs=P(None, "dp", None), check_vma=False
    )
```

```python
import functools
import jax
import jax.numpy as jnp
from jax import lax
from jax.experimental import pallas as pl
from jax.experimental.pallas import tpu as pltpu
from jax.sharding import PartitionSpec as P

F32 = jnp.float32
BF16 = jnp.bfloat16
MESH = pl.DeviceIdType.MESH
HI = lax.Precision.HIGHEST
BLOCK = 128
WIDE = 256
TILE = 8


def remote(src, dst, send, recv, where):
    return pltpu.make_async_remote_copy(
        src_ref=src, dst_ref=dst, send_sem=send, recv_sem=recv,
        device_id=where, device_id_type=MESH,
    )


def gather_kernel(n, direct, a_ref, b_ref, gx, gy, loc, s1, r1, s2, r2, s3, r3):
    me = lax.axis_index("dp")
    m = lax.axis_index("mp")
    half = n // 2
    pair, side = me // 2, me % 2
    sibling = pair * 2 + 1 - side
    barrier = pltpu.get_barrier_semaphore()
    for s in range(1, n):
        pl.semaphore_signal(barrier, inc=1, device_id=((me + s) % n, m), device_id_type=MESH)
    pl.semaphore_wait(barrier, n - 1)

    def begin(x, part):
        for s in range(1, half):
            peer = ((pair + s) % half) * 2 + side
            remote(x, gx.at[me], s1.at[s], r1.at[s], (peer, m)).start()
        remote(x, gx.at[me], s1.at[0], r1.at[0], (sibling, m)).start()
        for s in range(1, n):
            peer = (me + s) % n
            remote(part(peer), gy.at[me], s3.at[s], r3.at[s], (peer, m)).start()
        pltpu.make_async_copy(x, gx.at[me], loc.at[0]).start()
        pltpu.make_async_copy(part(me), gy.at[me], loc.at[1]).start()

    if direct:
        layer = m // 2
        rw = gy.shape[2]

        def columns(ref):
            return lambda j: ref.at[layer, :, pl.ds(pl.multiple_of(j * rw, rw), rw)]

        @pl.when(m % 2 == 0)
        def _():
            begin(a_ref.at[layer], columns(b_ref))

        @pl.when(m % 2 == 1)
        def _():
            begin(b_ref.at[layer], columns(a_ref))
    else:
        begin(a_ref, lambda j: b_ref.at[j])

    x = gx.at[me]
    for s in range(1, half):
        origin = ((pair - s + half) % half) * 2 + side
        remote(x, gx.at[origin], s1.at[s], r1.at[s], (sibling, m)).wait_recv()
        remote(gx.at[origin], gx.at[origin], s2.at[s], r2.at[s], (sibling, m)).start()
    remote(x, gx.at[sibling], s1.at[0], r1.at[0], (sibling, m)).wait_recv()
    for s in range(1, half):
        origin = ((pair - s + half) % half) * 2 + 1 - side
        remote(x, gx.at[origin], s2.at[s], r2.at[s], (sibling, m)).wait_recv()
    for s in range(1, n):
        origin = (me - s + n) % n
        remote(gy.at[me], gy.at[origin], s3.at[s], r3.at[s], (origin, m)).wait_recv()
    for s in range(half):
        remote(x, x, s1.at[s], r1.at[s], (sibling, m)).wait_send()
    for s in range(1, half):
        remote(x, x, s2.at[s], r2.at[s], (sibling, m)).wait_send()
    for s in range(1, n):
        remote(gy.at[me], gy.at[me], s3.at[s], r3.at[s], (sibling, m)).wait_send()
    pltpu.make_async_copy(x, x, loc.at[0]).wait()
    pltpu.make_async_copy(gy.at[me], gy.at[me], loc.at[1]).wait()


def gather(n, direct, x, y):
    any_space = pl.BlockSpec(memory_space=pl.ANY)
    dma = pltpu.SemaphoreType.DMA
    return pl.pallas_call(
        functools.partial(gather_kernel, n, direct),
        out_shape=[
            jax.ShapeDtypeStruct((n,) + x.shape[-2:], x.dtype),
            jax.ShapeDtypeStruct((n, x.shape[-2], x.shape[-1] // n), y.dtype),
        ],
        in_specs=[any_space] * 2,
        out_specs=[any_space] * 2,
        scratch_shapes=[dma((2,)), dma((n,)), dma((n,)), dma((n,)), dma((n,)), dma((n,)), dma((n,))],
        compiler_params=pltpu.CompilerParams(collective_id=0, has_side_effects=True),
        name="gather_sources",
    )(x, y)


def sweep_block(tiles):
    width = tiles[0].shape[1]
    shape = (TILE, width)
    lane = lax.broadcasted_iota(jnp.int32, shape, 1)
    sub = lax.broadcasted_iota(jnp.int32, shape, 0)
    idx = range(TILE)
    for g in range(width // TILE):
        first = g * TILE
        inside = (lane >= first) & (lane < first + TILE)
        rows = [jnp.broadcast_to(tiles[g][i : i + 1, :], shape) for i in idx]
        s = {
            (i, j): jnp.broadcast_to(rows[i][:, first + j : first + j + 1], shape)
            for i in idx for j in idx if i <= j
        }

        def at(i, j):
            return (i, j) if i <= j else (j, i)

        for k in idx[::2]:
            h = k + 1
            inv = 1.0 / (s[k, k] * s[h, h] - s[k, h] * s[k, h])
            p00, p01, p11 = s[h, h] * inv, -s[k, h] * inv, s[k, k] * inv
            rest = [i for i in idx if i not in (k, h)]
            u = {i: s[at(i, k)] * p00 + s[at(i, h)] * p01 for i in rest}
            v = {i: s[at(i, k)] * p01 + s[at(i, h)] * p11 for i in rest}
            for i in rest:
                for j in rest:
                    if i <= j:
                        s[i, j] = s[i, j] - (s[at(i, k)] * u[j] + s[at(i, h)] * v[j])
            for i in rest:
                s[at(i, k)] = u[i]
                s[at(i, h)] = v[i]
            s[k, k], s[k, h], s[h, h] = -p00, -p01, -p11
        rows = [
            jnp.where(inside, jnp.where(lane == first + i, -1.0, 0.0), rows[i]) for i in idx
        ]
        scaled = []
        for i in idx:
            terms = [s[at(i, j)] * rows[j] for j in idx]
            while len(terms) > 1:
                terms = [x + y for x, y in zip(terms[0::2], terms[1::2])]
            scaled.append(-terms[0])
        out = []
        for t, tile in enumerate(tiles):
            if t == g:
                fresh = scaled[0]
                for i in idx[1:]:
                    fresh = jnp.where(sub == i, scaled[i], fresh)
                out.append(fresh)
                continue
            terms = [
                jnp.broadcast_to(tile[:, first + i : first + i + 1], shape) * scaled[i] for i in idx
            ]
            while len(terms) > 1:
                terms = [x + y for x, y in zip(terms[0::2], terms[1::2])]
            out.append(jnp.where(inside, 0.0, tile) - terms[0])
        tiles = out
    return tiles


def split(x):
    first = x.astype(BF16)
    left = x - first.astype(F32)
    second = left.astype(BF16)
    return first, second, (left - second.astype(F32)).astype(BF16)


def invert_kernel(refreshed, shift, factor, kept, out, a, r, p, left, right):
    width = factor.shape[0]
    steps = width // BLOCK
    row_id = lax.broadcasted_iota(jnp.int32, (BLOCK, width), 0)
    col_id = lax.broadcasted_iota(jnp.int32, (BLOCK, width), 1)

    @pl.loop(0, steps)
    def _(i):
        rows = pl.ds(pl.multiple_of(i * BLOCK, BLOCK), BLOCK)
        a[rows, :] = factor[rows, :] + jnp.where(row_id + i * BLOCK == col_id, shift[0], 0.0)

    @pl.loop(0, steps)
    def _(k):
        ks = pl.ds(pl.multiple_of(k * BLOCK, BLOCK), BLOCK)
        block = a[ks, ks]
        tiles = [block[t * TILE : (t + 1) * TILE, :] for t in range(BLOCK // TILE)]
        tiles = sweep_block(tiles)
        for t, tile in enumerate(tiles):
            p[t * TILE : (t + 1) * TILE, :] = tile
        r[...] = -jnp.dot(p[...], a[ks, :], precision=HI, preferred_element_type=F32)
        r[:, ks] = p[...]

        c = split(a[:, ks])
        q = split(r[...])
        for t, (i, j) in enumerate(((0, 2), (2, 0), (1, 1), (0, 1), (1, 0), (0, 0))):
            left[:, t * BLOCK : (t + 1) * BLOCK] = c[i]
            right[t * BLOCK : (t + 1) * BLOCK, :] = q[j]
        a[:, ks] = jnp.zeros((width, BLOCK), F32)

        @pl.loop(0, width // WIDE)
        def _(i):
            cols = pl.ds(pl.multiple_of(i * WIDE, WIDE), WIDE)
            a[:, cols] = a[:, cols] - jnp.dot(left[...], right[:, cols], preferred_element_type=F32)

        a[ks, :] = r[...]

    fresh = refreshed[0] > 0

    @pl.loop(0, steps)
    def _(i):
        rows = pl.ds(pl.multiple_of(i * BLOCK, BLOCK), BLOCK)
        out[rows, :] = jnp.where(fresh, -a[rows, :], kept[rows, :].astype(F32)).astype(BF16)


def invert(refreshed, shift, factor, kept):
    width = factor.shape[0]
    smem = pl.BlockSpec(memory_space=pltpu.SMEM)
    vmem = pl.BlockSpec(memory_space=pltpu.VMEM)
    return pl.pallas_call(
        invert_kernel,
        out_shape=jax.ShapeDtypeStruct((width, width), BF16),
        in_specs=[smem, smem, vmem, vmem],
        out_specs=vmem,
        scratch_shapes=[
            pltpu.VMEM((width, width), F32),
            pltpu.VMEM((BLOCK, width), F32),
            pltpu.VMEM((BLOCK, BLOCK), F32),
            pltpu.VMEM((width, 6 * BLOCK), BF16),
            pltpu.VMEM((6 * BLOCK, width), BF16),
        ],
        compiler_params=pltpu.CompilerParams(vmem_limit_bytes=40 * 1024 * 1024),
        name="invert_damped",
    )(refreshed, shift, factor, kept)


def apply_kernel(n, parts, inv, grad, step, out, b, got, done, s1, r1, s2, r2):
    me = lax.axis_index("dp")
    m = lax.axis_index("mp")
    other = m + 1 - 2 * (m % 2)
    width = inv.shape[0]
    rw = width // n
    is_out = m % 2
    barrier = pltpu.get_barrier_semaphore()
    for j in range(n):
        pl.semaphore_signal(barrier, inc=1, device_id=(j, other), device_id_type=MESH)
    for q in range(1, parts):
        pl.semaphore_signal(barrier, inc=1, device_id=(me, (m + q) % parts), device_id_type=MESH)
    pl.semaphore_wait(barrier, n + parts - 1)

    b[...] = jnp.dot(inv[...], grad[...], preferred_element_type=F32).astype(BF16).reshape(n, rw, rw)
    for s in range(n):
        j = (me + s) % n

        @pl.when(is_out == 1)
        def _():
            remote(b.at[j], got.at[me], s1.at[s], r1.at[s], (j, other)).start()

    @pl.when(is_out == 0)
    def _():
        for s in range(n):
            origin = (me - s + n) % n
            remote(b.at[origin], got.at[origin], s1.at[s], r1.at[s], (origin, other)).wait_recv()
        total = jnp.zeros((rw, width), F32)
        for j in range(n):
            total = total + jnp.dot(got[j], inv[j * rw : (j + 1) * rw, :], preferred_element_type=F32)
        done[m // 2] = (total * step[m // 2]).astype(BF16)

    chunks = max(1, min(4, rw // 16))
    size = rw // chunks

    def hop(layer, c, way, where):
        part = done.at[layer, pl.ds(c * size, size)]
        return remote(part, part, s2.at[layer, way, c], r2.at[layer, c], (me, where))

    up, down = m + 1, m - 1
    for c in range(chunks):
        for s in range(0, parts, 2):
            layer = s // 2

            @pl.when((m == s) & (up < parts))
            def _():
                hop(layer, c, 0, up).start()

            @pl.when((m == s) & (down >= 0))
            def _():
                hop(layer, c, 1, down).start()

    for c in range(chunks):
        for s in range(0, parts, 2):
            layer = s // 2

            @pl.when(m != s)
            def _():
                hop(layer, c, 0, other).wait_recv()

            @pl.when((m > s) & (up < parts))
            def _():
                hop(layer, c, 0, up).start()

            @pl.when((m < s) & (down >= 0))
            def _():
                hop(layer, c, 1, down).start()

    for c in range(chunks):
        for s in range(0, parts, 2):
            layer = s // 2

            @pl.when((m >= s) & (up < parts))
            def _():
                hop(layer, c, 0, other).wait_send()

            @pl.when((m <= s) & (down >= 0))
            def _():
                hop(layer, c, 1, other).wait_send()

    @pl.when(is_out == 1)
    def _():
        for s in range(n):
            j = (me + s) % n
            remote(b.at[j], got.at[me], s1.at[s], r1.at[s], (j, other)).wait_send()

    out[...] = done[...]


def apply(n, parts, inv, grad, step):
    width = inv.shape[0]
    rw = width // n
    layers = step.shape[0]
    vmem = pl.BlockSpec(memory_space=pltpu.VMEM)
    dma = pltpu.SemaphoreType.DMA
    return pl.pallas_call(
        functools.partial(apply_kernel, n, parts),
        out_shape=jax.ShapeDtypeStruct((layers, rw, width), BF16),
        in_specs=[vmem, vmem, pl.BlockSpec(memory_space=pltpu.SMEM)],
        out_specs=vmem,
        scratch_shapes=[
            pltpu.VMEM((n, rw, rw), BF16),
            pltpu.VMEM((n, rw, rw), BF16),
            pltpu.VMEM((layers, rw, width), BF16),
            dma((n,)), dma((n,)), dma((layers, 2, 4)), dma((layers, 4)),
        ],
        compiler_params=pltpu.CompilerParams(
            collective_id=1, has_side_effects=True, vmem_limit_bytes=32 * 1024 * 1024
        ),
        name="apply_inverses",
    )(inv, grad, step)


def body(layer_inputs, out_grads, damping, owners, old_inverse, step_size):
    parts = lax.axis_size("mp")
    n = lax.axis_size("dp")
    m = lax.axis_index("mp")
    tokens = layer_inputs.shape[1]
    width = layer_inputs.shape[2]
    count_all = tokens * n
    rw = width // n
    direct = rw % 128 == 0
    if direct:
        mine, other = layer_inputs, out_grads
    else:
        xs = lax.dynamic_index_in_dim(layer_inputs, m // 2, 0, keepdims=False)
        gs = lax.dynamic_index_in_dim(out_grads, m // 2, 0, keepdims=False)
        even = m % 2 == 0
        mine = jnp.where(even, xs, gs)
        other = jnp.where(even, gs, xs).reshape(tokens, n, rw).transpose(1, 0, 2)
    source, columns = gather(n, direct, mine, other)
    source = source.reshape(count_all, width)
    columns = columns.reshape(count_all, rw)
    dims = (((0,), (0,)), ((), ()))
    factor = lax.dot_general(source, source, dims, preferred_element_type=F32) / count_all
    grad = (lax.dot_general(source, columns, dims, preferred_element_type=F32) / count_all).astype(BF16)
    refreshed = (owners[m] < n).astype(jnp.int32).reshape(1)
    shift = damping[m].reshape(1)
    inverse = invert(refreshed, shift, factor, old_inverse[0])
    return apply(n, parts, inverse, grad, step_size)


def solution(mesh):
    placed = (P(None, "dp", None), P(None, "dp", None), P(), P(), P("mp", None, None), P())
    return jax.shard_map(
        body, mesh=mesh, in_specs=placed, out_specs=P(None, "dp", None), check_vma=False
    )
```

```python
import functools
import jax
import jax.numpy as jnp
from jax import lax
from jax.experimental import pallas as pl
from jax.experimental.pallas import tpu as pltpu
from jax.sharding import PartitionSpec as P

F32 = jnp.float32
BF16 = jnp.bfloat16
MESH = pl.DeviceIdType.MESH
HI = lax.Precision.HIGHEST
BLOCK = 128
WIDE = 256
TILE = 8


def remote(src, dst, send, recv, where):
    return pltpu.make_async_remote_copy(
        src_ref=src, dst_ref=dst, send_sem=send, recv_sem=recv,
        device_id=where, device_id_type=MESH,
    )


def gather_kernel(n, direct, a_ref, b_ref, gx, gy, loc, s1, r1, s2, r2, s3, r3):
    me = lax.axis_index("dp")
    m = lax.axis_index("mp")
    half = n // 2
    pair, side = me // 2, me % 2
    sibling = pair * 2 + 1 - side
    barrier = pltpu.get_barrier_semaphore()
    for s in range(1, n):
        pl.semaphore_signal(barrier, inc=1, device_id=((me + s) % n, m), device_id_type=MESH)
    pl.semaphore_wait(barrier, n - 1)

    def begin(x, part):
        for s in range(1, half):
            peer = ((pair + s) % half) * 2 + side
            remote(x, gx.at[me], s1.at[s], r1.at[s], (peer, m)).start()
        remote(x, gx.at[me], s1.at[0], r1.at[0], (sibling, m)).start()
        for s in range(1, n):
            peer = (me + s) % n
            remote(part(peer), gy.at[me], s3.at[s], r3.at[s], (peer, m)).start()
        pltpu.make_async_copy(x, gx.at[me], loc.at[0]).start()
        pltpu.make_async_copy(part(me), gy.at[me], loc.at[1]).start()

    if direct:
        layer = m // 2
        rw = gy.shape[2]

        def columns(ref):
            return lambda j: ref.at[layer, :, pl.ds(pl.multiple_of(j * rw, rw), rw)]

        @pl.when(m % 2 == 0)
        def _():
            begin(a_ref.at[layer], columns(b_ref))

        @pl.when(m % 2 == 1)
        def _():
            begin(b_ref.at[layer], columns(a_ref))
    else:
        begin(a_ref, lambda j: b_ref.at[j])

    x = gx.at[me]
    for s in range(1, half):
        origin = ((pair - s + half) % half) * 2 + side
        remote(x, gx.at[origin], s1.at[s], r1.at[s], (sibling, m)).wait_recv()
        remote(gx.at[origin], gx.at[origin], s2.at[s], r2.at[s], (sibling, m)).start()
    remote(x, gx.at[sibling], s1.at[0], r1.at[0], (sibling, m)).wait_recv()
    for s in range(1, half):
        origin = ((pair - s + half) % half) * 2 + 1 - side
        remote(x, gx.at[origin], s2.at[s], r2.at[s], (sibling, m)).wait_recv()
    for s in range(1, n):
        origin = (me - s + n) % n
        remote(gy.at[me], gy.at[origin], s3.at[s], r3.at[s], (origin, m)).wait_recv()
    for s in range(half):
        remote(x, x, s1.at[s], r1.at[s], (sibling, m)).wait_send()
    for s in range(1, half):
        remote(x, x, s2.at[s], r2.at[s], (sibling, m)).wait_send()
    for s in range(1, n):
        remote(gy.at[me], gy.at[me], s3.at[s], r3.at[s], (sibling, m)).wait_send()
    pltpu.make_async_copy(x, x, loc.at[0]).wait()
    pltpu.make_async_copy(gy.at[me], gy.at[me], loc.at[1]).wait()


def square_gather_kernel(n, a_ref, b_ref, gx, gy, loc, s1, r1, s2, r2, s3, r3):
    me = lax.axis_index("dp")
    m = lax.axis_index("mp")
    beside = m + 1 - 2 * (m % 2)
    layer = m // 2
    pair, side = me // 2, me % 2
    px = pair + 1 - 2 * (pair % 2)
    py = (pair + 2) % 4
    pd = (px + 2) % 4
    sibling = pair * 2 + 1 - side
    near_x, near_y, far = px * 2 + side, py * 2 + side, pd * 2 + side
    half = gx.shape[1] // 2
    rw = gy.shape[2]
    cols = pl.ds(pl.multiple_of(me * rw, rw), rw)
    barrier = pltpu.get_barrier_semaphore()
    for s in range(1, n):
        pl.semaphore_signal(barrier, inc=1, device_id=((me + s) % n, m), device_id_type=MESH)
    pl.semaphore_signal(barrier, inc=1, device_id=(me, beside), device_id_type=MESH)
    pl.semaphore_wait(barrier, n)

    def begin(x):
        remote(x, gx.at[me], s1.at[1], r1.at[1], (near_x, m)).start()
        remote(x, gx.at[me], s1.at[2], r1.at[2], (near_y, m)).start()
        remote(x, gx.at[me], s1.at[0], r1.at[0], (sibling, m)).start()
        pltpu.make_async_copy(x, gx.at[me], loc.at[0]).start()

    @pl.when(m % 2 == 0)
    def _():
        begin(a_ref.at[layer])
        remote(a_ref.at[layer, :, cols], gy.at[me], s3.at[0], r3.at[0], (me, beside)).start()

    @pl.when(m % 2 == 1)
    def _():
        begin(b_ref.at[layer])

    def whole(origin):
        return gx.at[origin]

    def part(origin, h):
        return gx.at[origin, pl.ds(h * half, half)]

    def arrive(block, sems, k):
        remote(block, block, s1.at[0], sems.at[k], (sibling, m)).wait_recv()

    def forward(block, k, peer):
        remote(block, block, s2.at[k], r2.at[k], (peer, m)).start()

    def columns(e, origin):
        @pl.when(m % 2 == 0)
        def _():
            remote(gx.at[origin, :, cols], gy.at[origin], s3.at[e], r3.at[e], (me, beside)).start()

    arrive(whole(sibling), r1, 0)
    columns(1, sibling)
    arrive(whole(near_x), r1, 1)
    forward(part(near_x, 0), 5, near_y)
    forward(whole(near_x), 1, sibling)
    columns(2, near_x)
    arrive(whole(near_y), r1, 2)
    forward(part(near_y, 1), 6, near_x)
    forward(whole(near_y), 2, sibling)
    columns(4, near_y)
    other_x, other_y, other_far = px * 2 + 1 - side, py * 2 + 1 - side, pd * 2 + 1 - side
    arrive(whole(other_x), r2, 1)
    columns(3, other_x)
    arrive(whole(other_y), r2, 2)
    columns(5, other_y)
    arrive(part(far, 0), r2, 5)
    forward(part(far, 0), 3, sibling)
    arrive(part(far, 1), r2, 6)
    forward(part(far, 1), 4, sibling)
    columns(6, far)
    arrive(part(other_far, 0), r2, 3)
    arrive(part(other_far, 1), r2, 4)
    columns(7, other_far)
    order = (me, sibling, near_x, other_x, near_y, other_y, far, other_far)

    @pl.when(m % 2 == 1)
    def _():
        for e, origin in enumerate(order):
            remote(gy.at[origin], gy.at[origin], s3.at[e], r3.at[e], (me, beside)).wait_recv()

    @pl.when(m % 2 == 0)
    def _():
        for e, origin in enumerate(order):
            remote(gx.at[origin, :, cols], gy.at[origin], s3.at[e], r3.at[e], (me, beside)).wait_send()

    for k in range(3):
        remote(whole(me), whole(me), s1.at[k], r1.at[k], (sibling, m)).wait_send()
    for k, block in (
        (1, whole(near_x)), (2, whole(near_y)), (3, part(far, 0)), (4, part(far, 1)),
        (5, part(near_x, 0)), (6, part(near_y, 1)),
    ):
        remote(block, block, s2.at[k], r2.at[k], (sibling, m)).wait_send()
    pltpu.make_async_copy(whole(me), whole(me), loc.at[0]).wait()


def gather(n, direct, x, y):
    square = direct and n == 8 and x.shape[-2] % 32 == 0
    any_space = pl.BlockSpec(memory_space=pl.ANY)
    dma = pltpu.SemaphoreType.DMA
    return pl.pallas_call(
        functools.partial(square_gather_kernel, n) if square else functools.partial(gather_kernel, n, direct),
        out_shape=[
            jax.ShapeDtypeStruct((n,) + x.shape[-2:], x.dtype),
            jax.ShapeDtypeStruct((n, x.shape[-2], x.shape[-1] // n), y.dtype),
        ],
        in_specs=[any_space] * 2,
        out_specs=[any_space] * 2,
        scratch_shapes=[dma((2,)), dma((n,)), dma((n,)), dma((n,)), dma((n,)), dma((n,)), dma((n,))],
        compiler_params=pltpu.CompilerParams(collective_id=0, has_side_effects=True),
        name="gather_sources",
    )(x, y)


def sweep_block(tiles):
    width = tiles[0].shape[1]
    shape = (TILE, width)
    lane = lax.broadcasted_iota(jnp.int32, shape, 1)
    sub = lax.broadcasted_iota(jnp.int32, shape, 0)
    idx = range(TILE)
    for g in range(width // TILE):
        first = g * TILE
        inside = (lane >= first) & (lane < first + TILE)
        rows = [jnp.broadcast_to(tiles[g][i : i + 1, :], shape) for i in idx]
        s = {
            (i, j): jnp.broadcast_to(rows[i][:, first + j : first + j + 1], shape)
            for i in idx for j in idx if i <= j
        }

        def at(i, j):
            return (i, j) if i <= j else (j, i)

        for k in idx[::2]:
            h = k + 1
            inv = 1.0 / (s[k, k] * s[h, h] - s[k, h] * s[k, h])
            p00, p01, p11 = s[h, h] * inv, -s[k, h] * inv, s[k, k] * inv
            rest = [i for i in idx if i not in (k, h)]
            u = {i: s[at(i, k)] * p00 + s[at(i, h)] * p01 for i in rest}
            v = {i: s[at(i, k)] * p01 + s[at(i, h)] * p11 for i in rest}
            for i in rest:
                for j in rest:
                    if i <= j:
                        s[i, j] = s[i, j] - (s[at(i, k)] * u[j] + s[at(i, h)] * v[j])
            for i in rest:
                s[at(i, k)] = u[i]
                s[at(i, h)] = v[i]
            s[k, k], s[k, h], s[h, h] = -p00, -p01, -p11
        rows = [
            jnp.where(inside, jnp.where(lane == first + i, -1.0, 0.0), rows[i]) for i in idx
        ]
        scaled = []
        for i in idx:
            terms = [s[at(i, j)] * rows[j] for j in idx]
            while len(terms) > 1:
                terms = [x + y for x, y in zip(terms[0::2], terms[1::2])]
            scaled.append(-terms[0])
        out = []
        for t, tile in enumerate(tiles):
            if t == g:
                fresh = scaled[0]
                for i in idx[1:]:
                    fresh = jnp.where(sub == i, scaled[i], fresh)
                out.append(fresh)
                continue
            terms = [
                jnp.broadcast_to(tile[:, first + i : first + i + 1], shape) * scaled[i] for i in idx
            ]
            while len(terms) > 1:
                terms = [x + y for x, y in zip(terms[0::2], terms[1::2])]
            out.append(jnp.where(inside, 0.0, tile) - terms[0])
        tiles = out
    return tiles


def split(x):
    first = x.astype(BF16)
    left = x - first.astype(F32)
    second = left.astype(BF16)
    return first, second, (left - second.astype(F32)).astype(BF16)


def invert_kernel(refreshed, shift, factor, kept, out, a, r, p, left, right):
    width = factor.shape[0]
    steps = width // BLOCK
    row_id = lax.broadcasted_iota(jnp.int32, (BLOCK, width), 0)
    col_id = lax.broadcasted_iota(jnp.int32, (BLOCK, width), 1)

    @pl.loop(0, steps)
    def _(i):
        rows = pl.ds(pl.multiple_of(i * BLOCK, BLOCK), BLOCK)
        a[rows, :] = factor[rows, :] + jnp.where(row_id + i * BLOCK == col_id, shift[0], 0.0)

    @pl.loop(0, steps)
    def _(k):
        ks = pl.ds(pl.multiple_of(k * BLOCK, BLOCK), BLOCK)
        block = a[ks, ks]
        tiles = [block[t * TILE : (t + 1) * TILE, :] for t in range(BLOCK // TILE)]
        tiles = sweep_block(tiles)
        for t, tile in enumerate(tiles):
            p[t * TILE : (t + 1) * TILE, :] = tile
        r[...] = -jnp.dot(p[...], a[ks, :], precision=HI, preferred_element_type=F32)
        r[:, ks] = p[...]

        c = split(a[:, ks])
        q = split(r[...])
        for t, (i, j) in enumerate(((0, 2), (2, 0), (1, 1), (0, 1), (1, 0), (0, 0))):
            left[:, t * BLOCK : (t + 1) * BLOCK] = c[i]
            right[t * BLOCK : (t + 1) * BLOCK, :] = q[j]
        a[:, ks] = jnp.zeros((width, BLOCK), F32)

        @pl.loop(0, width // WIDE)
        def _(i):
            cols = pl.ds(pl.multiple_of(i * WIDE, WIDE), WIDE)
            a[:, cols] = a[:, cols] - jnp.dot(left[...], right[:, cols], preferred_element_type=F32)

        a[ks, :] = r[...]

    fresh = refreshed[0] > 0

    @pl.loop(0, steps)
    def _(i):
        rows = pl.ds(pl.multiple_of(i * BLOCK, BLOCK), BLOCK)
        out[rows, :] = jnp.where(fresh, -a[rows, :], kept[rows, :].astype(F32)).astype(BF16)


def invert(refreshed, shift, factor, kept):
    width = factor.shape[0]
    smem = pl.BlockSpec(memory_space=pltpu.SMEM)
    vmem = pl.BlockSpec(memory_space=pltpu.VMEM)
    return pl.pallas_call(
        invert_kernel,
        out_shape=jax.ShapeDtypeStruct((width, width), BF16),
        in_specs=[smem, smem, vmem, vmem],
        out_specs=vmem,
        scratch_shapes=[
            pltpu.VMEM((width, width), F32),
            pltpu.VMEM((BLOCK, width), F32),
            pltpu.VMEM((BLOCK, BLOCK), F32),
            pltpu.VMEM((width, 6 * BLOCK), BF16),
            pltpu.VMEM((6 * BLOCK, width), BF16),
        ],
        compiler_params=pltpu.CompilerParams(vmem_limit_bytes=40 * 1024 * 1024),
        name="invert_damped",
    )(refreshed, shift, factor, kept)


def apply_kernel(n, parts, inv, grad, step, out, b, got, done, s1, r1, s2, r2):
    me = lax.axis_index("dp")
    m = lax.axis_index("mp")
    other = m + 1 - 2 * (m % 2)
    width = inv.shape[0]
    rw = width // n
    is_out = m % 2
    barrier = pltpu.get_barrier_semaphore()
    for j in range(n):
        pl.semaphore_signal(barrier, inc=1, device_id=(j, other), device_id_type=MESH)
    for q in range(1, parts):
        pl.semaphore_signal(barrier, inc=1, device_id=(me, (m + q) % parts), device_id_type=MESH)
    pl.semaphore_wait(barrier, n + parts - 1)

    b[...] = jnp.dot(inv[...], grad[...], preferred_element_type=F32).astype(BF16).reshape(n, rw, rw)
    for s in range(n):
        j = (me + s) % n

        @pl.when(is_out == 1)
        def _():
            remote(b.at[j], got.at[me], s1.at[s], r1.at[s], (j, other)).start()

    @pl.when(is_out == 0)
    def _():
        for s in range(n):
            origin = (me - s + n) % n
            remote(b.at[origin], got.at[origin], s1.at[s], r1.at[s], (origin, other)).wait_recv()
        total = jnp.zeros((rw, width), F32)
        for j in range(n):
            total = total + jnp.dot(got[j], inv[j * rw : (j + 1) * rw, :], preferred_element_type=F32)
        done[m // 2] = (total * step[m // 2]).astype(BF16)

    chunks = max(1, min(4, rw // 16))
    size = rw // chunks

    def hop(layer, c, way, where):
        part = done.at[layer, pl.ds(c * size, size)]
        return remote(part, part, s2.at[layer, way, c], r2.at[layer, c], (me, where))

    up, down = m + 1, m - 1
    for c in range(chunks):
        for s in range(0, parts, 2):
            layer = s // 2

            @pl.when((m == s) & (up < parts))
            def _():
                hop(layer, c, 0, up).start()

            @pl.when((m == s) & (down >= 0))
            def _():
                hop(layer, c, 1, down).start()

    for c in range(chunks):
        for s in range(0, parts, 2):
            layer = s // 2

            @pl.when(m != s)
            def _():
                hop(layer, c, 0, other).wait_recv()

            @pl.when((m > s) & (up < parts))
            def _():
                hop(layer, c, 0, up).start()

            @pl.when((m < s) & (down >= 0))
            def _():
                hop(layer, c, 1, down).start()

    for c in range(chunks):
        for s in range(0, parts, 2):
            layer = s // 2

            @pl.when((m >= s) & (up < parts))
            def _():
                hop(layer, c, 0, other).wait_send()

            @pl.when((m <= s) & (down >= 0))
            def _():
                hop(layer, c, 1, other).wait_send()

    @pl.when(is_out == 1)
    def _():
        for s in range(n):
            j = (me + s) % n
            remote(b.at[j], got.at[me], s1.at[s], r1.at[s], (j, other)).wait_send()

    out[...] = done[...]


def apply(n, parts, inv, grad, step):
    width = inv.shape[0]
    rw = width // n
    layers = step.shape[0]
    vmem = pl.BlockSpec(memory_space=pltpu.VMEM)
    dma = pltpu.SemaphoreType.DMA
    return pl.pallas_call(
        functools.partial(apply_kernel, n, parts),
        out_shape=jax.ShapeDtypeStruct((layers, rw, width), BF16),
        in_specs=[vmem, vmem, pl.BlockSpec(memory_space=pltpu.SMEM)],
        out_specs=vmem,
        scratch_shapes=[
            pltpu.VMEM((n, rw, rw), BF16),
            pltpu.VMEM((n, rw, rw), BF16),
            pltpu.VMEM((layers, rw, width), BF16),
            dma((n,)), dma((n,)), dma((layers, 2, 4)), dma((layers, 4)),
        ],
        compiler_params=pltpu.CompilerParams(
            collective_id=1, has_side_effects=True, vmem_limit_bytes=32 * 1024 * 1024
        ),
        name="apply_inverses",
    )(inv, grad, step)


def body(layer_inputs, out_grads, damping, owners, old_inverse, step_size):
    parts = lax.axis_size("mp")
    n = lax.axis_size("dp")
    m = lax.axis_index("mp")
    tokens = layer_inputs.shape[1]
    width = layer_inputs.shape[2]
    count_all = tokens * n
    rw = width // n
    direct = rw % 128 == 0
    if direct:
        mine, other = layer_inputs, out_grads
    else:
        xs = lax.dynamic_index_in_dim(layer_inputs, m // 2, 0, keepdims=False)
        gs = lax.dynamic_index_in_dim(out_grads, m // 2, 0, keepdims=False)
        even = m % 2 == 0
        mine = jnp.where(even, xs, gs)
        other = jnp.where(even, gs, xs).reshape(tokens, n, rw).transpose(1, 0, 2)
    source, columns = gather(n, direct, mine, other)
    source = source.reshape(count_all, width)
    columns = columns.reshape(count_all, rw)
    dims = (((0,), (0,)), ((), ()))
    factor = lax.dot_general(source, source, dims, preferred_element_type=F32) / count_all
    grad = (lax.dot_general(source, columns, dims, preferred_element_type=F32) / count_all).astype(BF16)
    refreshed = (owners[m] < n).astype(jnp.int32).reshape(1)
    shift = damping[m].reshape(1)
    inverse = invert(refreshed, shift, factor, old_inverse[0])
    return apply(n, parts, inverse, grad, step_size)


def solution(mesh):
    placed = (P(None, "dp", None), P(None, "dp", None), P(), P(), P("mp", None, None), P())
    return jax.shard_map(
        body, mesh=mesh, in_specs=placed, out_specs=P(None, "dp", None), check_vma=False
    )
```

```python
import functools
import jax
import jax.numpy as jnp
from jax import lax
from jax.experimental import pallas as pl
from jax.experimental.pallas import tpu as pltpu
from jax.sharding import PartitionSpec as P

F32 = jnp.float32
BF16 = jnp.bfloat16
MESH = pl.DeviceIdType.MESH
HI = lax.Precision.HIGHEST
BLOCK = 128
WIDE = 256
TILE = 8


def remote(src, dst, send, recv, where):
    return pltpu.make_async_remote_copy(
        src_ref=src, dst_ref=dst, send_sem=send, recv_sem=recv,
        device_id=where, device_id_type=MESH,
    )


def gather_kernel(n, direct, a_ref, b_ref, gx, gy, loc, s1, r1, s2, r2, s3, r3):
    me = lax.axis_index("dp")
    m = lax.axis_index("mp")
    half = n // 2
    pair, side = me // 2, me % 2
    sibling = pair * 2 + 1 - side
    barrier = pltpu.get_barrier_semaphore()
    for s in range(1, n):
        pl.semaphore_signal(barrier, inc=1, device_id=((me + s) % n, m), device_id_type=MESH)
    pl.semaphore_wait(barrier, n - 1)

    def begin(x, part):
        for s in range(1, half):
            peer = ((pair + s) % half) * 2 + side
            remote(x, gx.at[me], s1.at[s], r1.at[s], (peer, m)).start()
        remote(x, gx.at[me], s1.at[0], r1.at[0], (sibling, m)).start()
        for s in range(1, n):
            peer = (me + s) % n
            remote(part(peer), gy.at[me], s3.at[s], r3.at[s], (peer, m)).start()
        pltpu.make_async_copy(x, gx.at[me], loc.at[0]).start()
        pltpu.make_async_copy(part(me), gy.at[me], loc.at[1]).start()

    if direct:
        layer = m // 2
        rw = gy.shape[2]

        def columns(ref):
            return lambda j: ref.at[layer, :, pl.ds(pl.multiple_of(j * rw, rw), rw)]

        @pl.when(m % 2 == 0)
        def _():
            begin(a_ref.at[layer], columns(b_ref))

        @pl.when(m % 2 == 1)
        def _():
            begin(b_ref.at[layer], columns(a_ref))
    else:
        begin(a_ref, lambda j: b_ref.at[j])

    x = gx.at[me]
    for s in range(1, half):
        origin = ((pair - s + half) % half) * 2 + side
        remote(x, gx.at[origin], s1.at[s], r1.at[s], (sibling, m)).wait_recv()
        remote(gx.at[origin], gx.at[origin], s2.at[s], r2.at[s], (sibling, m)).start()
    remote(x, gx.at[sibling], s1.at[0], r1.at[0], (sibling, m)).wait_recv()
    for s in range(1, half):
        origin = ((pair - s + half) % half) * 2 + 1 - side
        remote(x, gx.at[origin], s2.at[s], r2.at[s], (sibling, m)).wait_recv()
    for s in range(1, n):
        origin = (me - s + n) % n
        remote(gy.at[me], gy.at[origin], s3.at[s], r3.at[s], (origin, m)).wait_recv()
    for s in range(half):
        remote(x, x, s1.at[s], r1.at[s], (sibling, m)).wait_send()
    for s in range(1, half):
        remote(x, x, s2.at[s], r2.at[s], (sibling, m)).wait_send()
    for s in range(1, n):
        remote(gy.at[me], gy.at[me], s3.at[s], r3.at[s], (sibling, m)).wait_send()
    pltpu.make_async_copy(x, x, loc.at[0]).wait()
    pltpu.make_async_copy(gy.at[me], gy.at[me], loc.at[1]).wait()


def square_gather_kernel(n, a_ref, b_ref, gx, gy, loc, s1, r1, s2, r2, s3, r3):
    me = lax.axis_index("dp")
    m = lax.axis_index("mp")
    beside = m + 1 - 2 * (m % 2)
    layer = m // 2
    pair, side = me // 2, me % 2
    px = pair + 1 - 2 * (pair % 2)
    py = (pair + 2) % 4
    pd = (px + 2) % 4
    sibling = pair * 2 + 1 - side
    near_x, near_y, far = px * 2 + side, py * 2 + side, pd * 2 + side
    half = gx.shape[1] // 2
    rw = gy.shape[2]
    cols = pl.ds(pl.multiple_of(me * rw, rw), rw)
    barrier = pltpu.get_barrier_semaphore()
    for s in range(1, n):
        pl.semaphore_signal(barrier, inc=1, device_id=((me + s) % n, m), device_id_type=MESH)
    pl.semaphore_signal(barrier, inc=1, device_id=(me, beside), device_id_type=MESH)
    pl.semaphore_wait(barrier, n)

    def begin(x):
        remote(x, gx.at[me], s1.at[1], r1.at[1], (near_x, m)).start()
        remote(x, gx.at[me], s1.at[2], r1.at[2], (near_y, m)).start()
        remote(x, gx.at[me], s1.at[0], r1.at[0], (sibling, m)).start()
        pltpu.make_async_copy(x, gx.at[me], loc.at[0]).start()

    @pl.when(m % 2 == 0)
    def _():
        begin(a_ref.at[layer])
        remote(a_ref.at[layer, :, cols], gy.at[me], s3.at[0], r3.at[0], (me, beside)).start()

    @pl.when(m % 2 == 1)
    def _():
        begin(b_ref.at[layer])

    def whole(origin):
        return gx.at[origin]

    def part(origin, h):
        return gx.at[origin, pl.ds(h * half, half)]

    def arrive(block, sems, k):
        remote(block, block, s1.at[0], sems.at[k], (sibling, m)).wait_recv()

    def forward(block, k, peer):
        remote(block, block, s2.at[k], r2.at[k], (peer, m)).start()

    def columns(e, origin):
        @pl.when(m % 2 == 0)
        def _():
            remote(gx.at[origin, :, cols], gy.at[origin], s3.at[e], r3.at[e], (me, beside)).start()

    arrive(whole(sibling), r1, 0)
    columns(1, sibling)
    arrive(whole(near_x), r1, 1)
    forward(part(near_x, 0), 5, near_y)
    forward(whole(near_x), 1, sibling)
    columns(2, near_x)
    arrive(whole(near_y), r1, 2)
    forward(part(near_y, 1), 6, near_x)
    forward(whole(near_y), 2, sibling)
    columns(4, near_y)
    other_x, other_y, other_far = px * 2 + 1 - side, py * 2 + 1 - side, pd * 2 + 1 - side
    arrive(whole(other_x), r2, 1)
    columns(3, other_x)
    arrive(whole(other_y), r2, 2)
    columns(5, other_y)
    arrive(part(far, 0), r2, 5)
    forward(part(far, 0), 3, sibling)
    arrive(part(far, 1), r2, 6)
    forward(part(far, 1), 4, sibling)
    columns(6, far)
    arrive(part(other_far, 0), r2, 3)
    arrive(part(other_far, 1), r2, 4)
    columns(7, other_far)
    order = (me, sibling, near_x, other_x, near_y, other_y, far, other_far)

    @pl.when(m % 2 == 1)
    def _():
        for e, origin in enumerate(order):
            remote(gy.at[origin], gy.at[origin], s3.at[e], r3.at[e], (me, beside)).wait_recv()

    @pl.when(m % 2 == 0)
    def _():
        for e, origin in enumerate(order):
            remote(gx.at[origin, :, cols], gy.at[origin], s3.at[e], r3.at[e], (me, beside)).wait_send()

    for k in range(3):
        remote(whole(me), whole(me), s1.at[k], r1.at[k], (sibling, m)).wait_send()
    for k, block in (
        (1, whole(near_x)), (2, whole(near_y)), (3, part(far, 0)), (4, part(far, 1)),
        (5, part(near_x, 0)), (6, part(near_y, 1)),
    ):
        remote(block, block, s2.at[k], r2.at[k], (sibling, m)).wait_send()
    pltpu.make_async_copy(whole(me), whole(me), loc.at[0]).wait()


def gather(n, direct, x, y):
    square = direct and n == 8 and x.shape[-2] % 32 == 0
    any_space = pl.BlockSpec(memory_space=pl.ANY)
    dma = pltpu.SemaphoreType.DMA
    return pl.pallas_call(
        functools.partial(square_gather_kernel, n) if square else functools.partial(gather_kernel, n, direct),
        out_shape=[
            jax.ShapeDtypeStruct((n,) + x.shape[-2:], x.dtype),
            jax.ShapeDtypeStruct((n, x.shape[-2], x.shape[-1] // n), y.dtype),
        ],
        in_specs=[any_space] * 2,
        out_specs=[any_space] * 2,
        scratch_shapes=[dma((2,)), dma((n,)), dma((n,)), dma((n,)), dma((n,)), dma((n,)), dma((n,))],
        compiler_params=pltpu.CompilerParams(collective_id=0, has_side_effects=True),
        name="gather_sources",
    )(x, y)


def sweep_block(tiles):
    width = tiles[0].shape[1]
    shape = (TILE, width)
    lane = lax.broadcasted_iota(jnp.int32, shape, 1)
    sub = lax.broadcasted_iota(jnp.int32, shape, 0)
    idx = range(TILE)
    for g in range(width // TILE):
        first = g * TILE
        inside = (lane >= first) & (lane < first + TILE)
        rows = [jnp.broadcast_to(tiles[g][i : i + 1, :], shape) for i in idx]
        s = {
            (i, j): jnp.broadcast_to(rows[i][:, first + j : first + j + 1], shape)
            for i in idx for j in idx if i <= j
        }

        def at(i, j):
            return (i, j) if i <= j else (j, i)

        for k in idx[::2]:
            h = k + 1
            inv = 1.0 / (s[k, k] * s[h, h] - s[k, h] * s[k, h])
            p00, p01, p11 = s[h, h] * inv, -s[k, h] * inv, s[k, k] * inv
            rest = [i for i in idx if i not in (k, h)]
            u = {i: s[at(i, k)] * p00 + s[at(i, h)] * p01 for i in rest}
            v = {i: s[at(i, k)] * p01 + s[at(i, h)] * p11 for i in rest}
            for i in rest:
                for j in rest:
                    if i <= j:
                        s[i, j] = s[i, j] - (s[at(i, k)] * u[j] + s[at(i, h)] * v[j])
            for i in rest:
                s[at(i, k)] = u[i]
                s[at(i, h)] = v[i]
            s[k, k], s[k, h], s[h, h] = -p00, -p01, -p11
        rows = [
            jnp.where(inside, jnp.where(lane == first + i, -1.0, 0.0), rows[i]) for i in idx
        ]
        scaled = []
        for i in idx:
            terms = [s[at(i, j)] * rows[j] for j in idx]
            while len(terms) > 1:
                terms = [x + y for x, y in zip(terms[0::2], terms[1::2])]
            scaled.append(-terms[0])
        out = []
        for t, tile in enumerate(tiles):
            if t == g:
                fresh = scaled[0]
                for i in idx[1:]:
                    fresh = jnp.where(sub == i, scaled[i], fresh)
                out.append(fresh)
                continue
            terms = [
                jnp.broadcast_to(tile[:, first + i : first + i + 1], shape) * scaled[i] for i in idx
            ]
            while len(terms) > 1:
                terms = [x + y for x, y in zip(terms[0::2], terms[1::2])]
            out.append(jnp.where(inside, 0.0, tile) - terms[0])
        tiles = out
    return tiles


def split(x):
    first = x.astype(BF16)
    left = x - first.astype(F32)
    second = left.astype(BF16)
    return first, second, (left - second.astype(F32)).astype(BF16)


def invert_kernel(n, owners, damping, factor, kept, out, a, r, p, left, right):
    width = factor.shape[0]
    steps = width // BLOCK
    mine = lax.axis_index("mp")
    shift = damping[mine]
    fresh = owners[mine] < n
    row_id = lax.broadcasted_iota(jnp.int32, (BLOCK, width), 0)
    col_id = lax.broadcasted_iota(jnp.int32, (BLOCK, width), 1)

    @pl.loop(0, steps)
    def _(i):
        rows = pl.ds(pl.multiple_of(i * BLOCK, BLOCK), BLOCK)
        a[rows, :] = factor[rows, :] + jnp.where(row_id + i * BLOCK == col_id, shift, 0.0)

    @pl.loop(0, steps)
    def _(k):
        ks = pl.ds(pl.multiple_of(k * BLOCK, BLOCK), BLOCK)
        block = a[ks, ks]
        tiles = [block[t * TILE : (t + 1) * TILE, :] for t in range(BLOCK // TILE)]
        tiles = sweep_block(tiles)
        for t, tile in enumerate(tiles):
            p[t * TILE : (t + 1) * TILE, :] = tile
        r[...] = -jnp.dot(p[...], a[ks, :], precision=HI, preferred_element_type=F32)
        r[:, ks] = p[...]

        c = split(a[:, ks])
        q = split(r[...])
        for t, (i, j) in enumerate(((0, 2), (2, 0), (1, 1), (0, 1), (1, 0), (0, 0))):
            left[:, t * BLOCK : (t + 1) * BLOCK] = c[i]
            right[t * BLOCK : (t + 1) * BLOCK, :] = q[j]
        a[:, ks] = jnp.zeros((width, BLOCK), F32)

        @pl.loop(0, width // WIDE)
        def _(i):
            cols = pl.ds(pl.multiple_of(i * WIDE, WIDE), WIDE)
            a[:, cols] = a[:, cols] - jnp.dot(left[...], right[:, cols], preferred_element_type=F32)

        a[ks, :] = r[...]

    @pl.loop(0, steps)
    def _(i):
        rows = pl.ds(pl.multiple_of(i * BLOCK, BLOCK), BLOCK)
        out[rows, :] = jnp.where(fresh, -a[rows, :], kept[rows, :].astype(F32)).astype(BF16)


def invert(n, owners, damping, factor, kept):
    width = factor.shape[0]
    smem = pl.BlockSpec(memory_space=pltpu.SMEM)
    vmem = pl.BlockSpec(memory_space=pltpu.VMEM)
    return pl.pallas_call(
        functools.partial(invert_kernel, n),
        out_shape=jax.ShapeDtypeStruct((width, width), BF16),
        in_specs=[smem, smem, vmem, vmem],
        out_specs=vmem,
        scratch_shapes=[
            pltpu.VMEM((width, width), F32),
            pltpu.VMEM((BLOCK, width), F32),
            pltpu.VMEM((BLOCK, BLOCK), F32),
            pltpu.VMEM((width, 6 * BLOCK), BF16),
            pltpu.VMEM((6 * BLOCK, width), BF16),
        ],
        compiler_params=pltpu.CompilerParams(vmem_limit_bytes=40 * 1024 * 1024),
        name="invert_damped",
    )(owners, damping, factor, kept)


def apply_kernel(n, parts, inv, grad, step, out, b, got, done, s1, r1, s2, r2):
    me = lax.axis_index("dp")
    m = lax.axis_index("mp")
    other = m + 1 - 2 * (m % 2)
    width = inv.shape[0]
    rw = width // n
    is_out = m % 2
    barrier = pltpu.get_barrier_semaphore()
    for j in range(n):
        pl.semaphore_signal(barrier, inc=1, device_id=(j, other), device_id_type=MESH)
    for q in range(1, parts):
        pl.semaphore_signal(barrier, inc=1, device_id=(me, (m + q) % parts), device_id_type=MESH)
    pl.semaphore_wait(barrier, n + parts - 1)

    product = lax.dot_general(
        inv[...], grad[...], (((1,), (1,)), ((), ())), preferred_element_type=F32
    )
    b[...] = product.astype(BF16).reshape(n, rw, rw)
    for s in range(n):
        j = (me + s) % n

        @pl.when(is_out == 1)
        def _():
            remote(b.at[j], got.at[me], s1.at[s], r1.at[s], (j, other)).start()

    @pl.when(is_out == 0)
    def _():
        for s in range(n):
            origin = (me - s + n) % n
            remote(b.at[origin], got.at[origin], s1.at[s], r1.at[s], (origin, other)).wait_recv()
        total = jnp.zeros((rw, width), F32)
        for j in range(n):
            total = total + jnp.dot(got[j], inv[j * rw : (j + 1) * rw, :], preferred_element_type=F32)
        done[m // 2] = (total * step[m // 2]).astype(BF16)

    chunks = max(1, min(4, rw // 16))
    size = rw // chunks

    def hop(layer, c, way, where):
        part = done.at[layer, pl.ds(c * size, size)]
        return remote(part, part, s2.at[layer, way, c], r2.at[layer, c], (me, where))

    up, down = m + 1, m - 1
    for c in range(chunks):
        for s in range(0, parts, 2):
            layer = s // 2

            @pl.when((m == s) & (up < parts))
            def _():
                hop(layer, c, 0, up).start()

            @pl.when((m == s) & (down >= 0))
            def _():
                hop(layer, c, 1, down).start()

    for c in range(chunks):
        for s in range(0, parts, 2):
            layer = s // 2

            @pl.when(m != s)
            def _():
                hop(layer, c, 0, other).wait_recv()

            @pl.when((m > s) & (up < parts))
            def _():
                hop(layer, c, 0, up).start()

            @pl.when((m < s) & (down >= 0))
            def _():
                hop(layer, c, 1, down).start()

    for c in range(chunks):
        for s in range(0, parts, 2):
            layer = s // 2

            @pl.when((m >= s) & (up < parts))
            def _():
                hop(layer, c, 0, other).wait_send()

            @pl.when((m <= s) & (down >= 0))
            def _():
                hop(layer, c, 1, other).wait_send()

    @pl.when(is_out == 1)
    def _():
        for s in range(n):
            j = (me + s) % n
            remote(b.at[j], got.at[me], s1.at[s], r1.at[s], (j, other)).wait_send()

    out[...] = done[...]


def apply(n, parts, inv, grad, step):
    width = inv.shape[0]
    rw = width // n
    layers = step.shape[0]
    vmem = pl.BlockSpec(memory_space=pltpu.VMEM)
    dma = pltpu.SemaphoreType.DMA
    return pl.pallas_call(
        functools.partial(apply_kernel, n, parts),
        out_shape=jax.ShapeDtypeStruct((layers, rw, width), BF16),
        in_specs=[vmem, vmem, pl.BlockSpec(memory_space=pltpu.SMEM)],
        out_specs=vmem,
        scratch_shapes=[
            pltpu.VMEM((n, rw, rw), BF16),
            pltpu.VMEM((n, rw, rw), BF16),
            pltpu.VMEM((layers, rw, width), BF16),
            dma((n,)), dma((n,)), dma((layers, 2, 4)), dma((layers, 4)),
        ],
        compiler_params=pltpu.CompilerParams(
            collective_id=1, has_side_effects=True, vmem_limit_bytes=32 * 1024 * 1024
        ),
        name="apply_inverses",
    )(inv, grad, step)


def body(layer_inputs, out_grads, damping, owners, old_inverse, step_size):
    parts = lax.axis_size("mp")
    n = lax.axis_size("dp")
    m = lax.axis_index("mp")
    tokens = layer_inputs.shape[1]
    width = layer_inputs.shape[2]
    count_all = tokens * n
    rw = width // n
    direct = rw % 128 == 0
    if direct:
        mine, other = layer_inputs, out_grads
    else:
        xs = lax.dynamic_index_in_dim(layer_inputs, m // 2, 0, keepdims=False)
        gs = lax.dynamic_index_in_dim(out_grads, m // 2, 0, keepdims=False)
        even = m % 2 == 0
        mine = jnp.where(even, xs, gs)
        other = jnp.where(even, gs, xs).reshape(tokens, n, rw).transpose(1, 0, 2)
    source, columns = gather(n, direct, mine, other)
    source = source.reshape(count_all, width)
    columns = columns.reshape(count_all, rw)
    dims = (((0,), (0,)), ((), ()))
    factor = lax.dot_general(source, source, dims, preferred_element_type=F32) / count_all
    grad = (lax.dot_general(columns, source, dims, preferred_element_type=F32) / count_all).astype(BF16)
    inverse = invert(n, owners, damping, factor, old_inverse[0])
    return apply(n, parts, inverse, grad, step_size)


def solution(mesh):
    placed = (P(None, "dp", None), P(None, "dp", None), P(), P(), P("mp", None, None), P())
    return jax.shard_map(
        body, mesh=mesh, in_specs=placed, out_specs=P(None, "dp", None), check_vma=False
    )
```
